32 devices in a mesh: pipe: 4 (over x, core), dp: 2 (over y), tensor: 4 (over z).
Axes of the slice: x: 2, y: 2, z: 4, core: 2. Of those that a mesh axis runs over, the one named last changes fastest.
Arguments:
- section_input: bfloat16 [4, 128, 8192], P('pipe', 'dp'), may hold values from -6 to 6
- norm_gain: float32 [4, 8192], P('pipe'), may hold values from 0.1 to 1.9
- projection: bfloat16 [4, 8192, 4096], P('pipe', 'dp', 'tensor'), may hold values from -0.0625 to 0.0625
- upstream_grad: bfloat16 [4, 128, 4096], P('pipe', 'dp', 'tensor'), may hold values from -4 to 4
Outputs:
- shifted_output: bfloat16 [4, 128, 4096], P('pipe', 'dp', 'tensor')
- normed_grad: bfloat16 [4, 128, 8192], P('pipe', None, ('dp', 'tensor'))
The draws below stay inside these ranges and needn't reach their ends.
All inputs are finite; a program needn't handle non-finite values.
Results may differ from the reference program's by a relative error of at most 0.013.
Values may be sent and summed in bfloat16 or wider, within the bound.
A program may use at most 64 MiB of HBM per device.

```python
import jax
import jax.numpy as jnp
from jax import lax

D = 8192
DW = 4096
PIPE = 4
TOKENS = 128
N_DP = 2
N_TENSOR = 4


def block_levels(key, shape, shards, low, top_value):
    factor_of, own = 1.0, jax.random.fold_in(key, 6)
    for axis_at, parts in shards:
        heights = jnp.exp(jax.random.uniform(jax.random.fold_in(own, axis_at), (parts,), jnp.float32, low / len(shards), top_value / len(shards)))
        factor_of = factor_of * jnp.repeat(heights, shape[axis_at] // parts).reshape([-1 if axis == axis_at else 1 for axis in range(len(shape))])
    return factor_of


def centred(key, dims, width, reach, split=(), dtype=jnp.bfloat16):
    values = jax.random.normal(key, dims, jnp.float32) * width
    if len(split) > 0:
        values = block_levels(key, dims, split, -0.22, 0.18) * values
    return jnp.clip(values, min=-reach, max=reach).astype(dtype)


def setup_inputs(seed: int = 0) -> dict:
    key_of = jax.random.split(jax.random.key(seed), 5)
    return {
        "section_input": centred(key_of[0], (PIPE, TOKENS, D), 1.0, 6.0, ((0, 4), (1, 2))),
        "norm_gain": jnp.clip(1.0 + 0.18 * jax.random.normal(key_of[1], (PIPE, D), jnp.float32), 0.1, 1.9),
        "projection": centred(key_of[2], (PIPE, D, DW), D ** -0.5, 0.0625, ((0, 4), (1, 2), (2, 4))),
        "upstream_grad": centred(key_of[3], (PIPE, TOKENS, DW), 0.5, 4.0, ((0, 4), (1, 2), (2, 4))),
    }


def rounded_sum(partials):
    low = partials.astype(jnp.bfloat16)
    low = lax.optimization_barrier(low)
    return lax.optimization_barrier(jnp.sum(low.astype(jnp.float32), axis=0))

def one_layer(items):
    section_x, gain, weight, cot = items
    xf = section_x.astype(jnp.float32)
    meansq = lax.optimization_barrier(jnp.mean(xf * xf, axis=-1, keepdims=True))
    normed = (xf * lax.rsqrt(meansq + 1e-05) * gain).astype(jnp.bfloat16)
    rows = normed.shape[0]
    normed_groups = normed.astype(jnp.float32).reshape(rows, N_DP, D // N_DP)
    weight_groups = weight.astype(jnp.float32).reshape(N_DP, D // N_DP, DW)
    pre = rounded_sum(jnp.einsum('tgk,gkn->gtn', normed_groups, weight_groups))
    act, back = jax.vjp(jax.nn.gelu, pre)
    layer_out = (xf[:, :DW] + act).astype(jnp.bfloat16)
    pre_grad = back(cot.astype(jnp.float32))[0].astype(jnp.bfloat16)
    grad_groups = pre_grad.astype(jnp.float32).reshape(rows, N_TENSOR, DW // N_TENSOR)
    weight_cols = weight.astype(jnp.float32).reshape(D, N_TENSOR, DW // N_TENSOR)
    normed_grad = rounded_sum(jnp.einsum('tgk,dgk->gtd', grad_groups, weight_cols)).astype(jnp.bfloat16)
    return (layer_out, normed_grad)

def reference(section_input, norm_gain, projection, upstream_grad):
    layer_out, normed_grad = lax.map(one_layer, (section_input, norm_gain, projection, upstream_grad))
    shifted_output = jnp.roll(layer_out, 1, axis=0)
    return (shifted_output, normed_grad)
```

```python
import functools

import jax
import jax.numpy as jnp
from jax import lax
from jax.experimental import pallas as pl
from jax.experimental.pallas import tpu as pltpu
from jax.sharding import PartitionSpec as P

F32 = jnp.float32
BF16 = jnp.bfloat16
MESH = pl.DeviceIdType.MESH
NS = 4


def kernel(
    np_, nd, nt,
    x_ref, g_ref, w_ref, c_ref,
    sh_ref, ng_ref,
    xv, gv, wv, cv, rs, rsr, xr, acc, ps, pr, lo, pgv, pgr, gp, rb,
    lsem, wsem,
    st_s, st_r, x_s, x_r, p_s, p_r, g_s, g_r, sh_s, sh_r,
    a_s, a_r, r_s, r_r, c_s, c_r,
):
    p = lax.axis_index("pipe")
    d = lax.axis_index("dp")
    t = lax.axis_index("tensor")
    T, D = x_ref.shape[1], x_ref.shape[2]
    K, C = w_ref.shape[1], w_ref.shape[2]
    KC, KQ = K // NS, K // nt

    def remote(src, dst, ss, rsem, **dev):
        return pltpu.make_async_remote_copy(
            src_ref=src, dst_ref=dst, send_sem=ss, recv_sem=rsem,
            device_id=dev, device_id_type=MESH,
        )

    nxt, prv = lax.rem(p + 1, np_), lax.rem(p + np_ - 1, np_)
    barrier = pltpu.get_barrier_semaphore()
    for o in range(1, nd):
        pl.semaphore_signal(barrier, inc=1, device_id={"dp": lax.rem(d + o, nd)}, device_id_type=MESH)
    for o in range(1, nt):
        pl.semaphore_signal(barrier, inc=1, device_id={"tensor": lax.rem(t + o, nt)}, device_id_type=MESH)
    pl.semaphore_signal(barrier, inc=1, device_id={"pipe": nxt}, device_id_type=MESH)
    pl.semaphore_signal(barrier, inc=1, device_id={"pipe": prv}, device_id_type=MESH)

    cx = pltpu.make_async_copy(x_ref.at[0], xv, lsem.at[0])
    cg = pltpu.make_async_copy(g_ref, gv, lsem.at[1])
    cc = pltpu.make_async_copy(c_ref.at[0], cv, lsem.at[2])
    cx.start()
    cg.start()
    cws = [
        pltpu.make_async_copy(w_ref.at[0, pl.ds(k * KC, KC)], wv.at[pl.ds(k * KC, KC)], wsem.at[k])
        for k in range(NS)
    ]
    for cw in cws:
        cw.start()
    cc.start()

    pl.semaphore_wait(barrier, (nd - 1) + (nt - 1) + 2)

    xcp = []
    for k in range(NS):
        for o in range(1, nd):
            e = lax.rem(d + o, nd)
            cols = pl.ds(pl.multiple_of(e * K + k * KC, 128), KC)
            cp = remote(
                x_ref.at[0, :, cols], xr.at[o - 1, :, pl.ds(k * KC, KC)],
                x_s.at[o - 1, k], x_r.at[o - 1, k], dp=e,
            )
            cp.start()
            xcp.append(cp)

    cx.wait()
    ss = jnp.zeros((T, 1), F32)
    SC = D // 8
    for k in range(8):
        xf = xv[:, k * SC:(k + 1) * SC].astype(F32)
        ss = ss + jnp.sum(xf * xf, axis=-1, keepdims=True)
    scale = lax.rsqrt(ss * (1.0 / D) + 1e-05)
    rs[...] = jnp.broadcast_to(scale, rs.shape)
    stcp = []
    for o in range(1, nd):
        cp = remote(rs, rsr.at[o - 1], st_s.at[o - 1], st_r.at[o - 1], dp=lax.rem(d + o, nd))
        cp.start()
        stcp.append(cp)

    cg.wait()

    def gain(k):
        return gv[:, pl.ds(pl.multiple_of(d * K + k * KC, 128), KC)]

    for k in range(NS):
        xf = xv[:, pl.ds(pl.multiple_of(d * K + k * KC, 128), KC)].astype(F32)
        nb = (xf * rs[:, 0:1] * gain(k)).astype(BF16)
        cws[k].wait()
        part = jnp.dot(nb, wv[k * KC:(k + 1) * KC, :], preferred_element_type=F32)
        if k == 0:
            acc[0] = part
        else:
            acc[0] += part

    pcp = []
    for cp in stcp:
        cp.wait_recv()
    for k in range(NS):
        for o in range(1, nd):
            xcp[k * (nd - 1) + o - 1].wait_recv()
            xf = xr[o - 1, :, k * KC:(k + 1) * KC].astype(F32)
            nb = (xf * rsr[o - 1, :, 0:1] * gain(k)).astype(BF16)
            part = jnp.dot(nb, wv[k * KC:(k + 1) * KC, :], preferred_element_type=F32)
            if k == 0:
                acc[o] = part
            elif k < NS - 1:
                acc[o] += part
            else:
                ps[o - 1] = (acc[o] + part).astype(BF16)
                back = nd - o
                cp = remote(
                    ps.at[o - 1], pr.at[back - 1], p_s.at[back - 1], p_r.at[back - 1],
                    dp=lax.rem(d + back, nd),
                )
                cp.start()
                pcp.append(cp)
    for cp in pcp:
        cp.wait_recv()
    cc.wait()

    k0 = 0.7978845608028654
    k1 = 0.044715
    CB = 256
    for b in range(C // CB):
        cols = slice(b * CB, (b + 1) * CB)
        pre = acc[0, :, cols].astype(BF16).astype(F32)
        for o in range(1, nd):
            pre = pre + pr[o - 1, :, cols].astype(F32)
        sq = pre * pre
        th = jnp.tanh(k0 * (pre + k1 * (sq * pre)))
        cdf = 0.5 * (1.0 + th)
        slope = cdf + 0.5 * pre * ((1.0 - th * th) * (k0 * (1.0 + 3.0 * k1 * sq)))
        pgv[:, cols] = (cv[:, cols].astype(F32) * slope).astype(BF16)
        res = xv[:, pl.ds(pl.multiple_of(t * C + b * CB, 128), CB)].astype(F32)
        lo[:, cols] = (res + pre * cdf).astype(BF16)
    gcp = []
    for o in range(1, nd):
        cp = remote(pgv, pgr.at[o - 1], g_s.at[o - 1], g_r.at[o - 1], dp=lax.rem(d + o, nd))
        cp.start()
        gcp.append(cp)
    shcp = remote(lo, sh_ref.at[0], sh_s, sh_r, pipe=nxt)
    shcp.start()

    low = t < 2
    inner = jnp.where(low, 1, 2)
    outer = jnp.where(low, 0, 3)
    is_outer = t == outer
    is_inner = t == inner
    partner = inner + outer - t
    dests = [3 - outer, 3 - inner, partner, t]
    acp, rcp, ccp = [], [], []
    for s in range(nd):
        acp.append(remote(gp.at[s, 2], rb.at[s, 0], a_s.at[s], a_r.at[s], tensor=partner))
        rcp.append([remote(gp.at[s, j], rb.at[s, 2 + j], r_s.at[s, j], r_r.at[s, j], tensor=partner) for j in range(2)])
        ccp.append([remote(gp.at[s, j], rb.at[s, 1], c_s.at[s, j], c_r.at[s], tensor=dests[j]) for j in range(2)])
    for s in range(nd):
        if s:
            gcp[s - 1].wait_recv()
        for j in range(4):
            pg = pgr[s - 1] if s else pgv[...]
            wb = wv[pl.ds(pl.multiple_of(dests[j] * KQ, KQ), KQ), :]
            part = lax.dot_general(pg, wb, (((1,), (1,)), ((), ())), preferred_element_type=F32)
            gp[s, j] = part.astype(BF16)
            if j < 2:
                @pl.when(is_outer)
                def _():
                    rcp[s][j].start()
            elif j == 2:
                acp[s].start()

    @pl.when(is_inner)
    def _():
        for s in range(nd):
            for j in range(2):
                rcp[s][j].wait_recv()
                gp[s, j] = (gp[s, j].astype(F32) + rb[s, 2 + j].astype(F32)).astype(BF16)
                ccp[s][j].start()

    for s in range(nd):
        acp[s].wait_recv()
        ccp[s][0].wait_recv()
        src = lax.rem(d - s + nd, nd)
        ng_ref[0, pl.ds(pl.multiple_of(src * T, T), T), :] = (
            gp[s, 3].astype(F32) + rb[s, 0].astype(F32) + rb[s, 1].astype(F32)
        ).astype(BF16)

    for cp in xcp + stcp + pcp + gcp + acp:
        cp.wait_send()
    shcp.wait()

    @pl.when(is_outer)
    def _():
        for s in range(nd):
            for j in range(2):
                rcp[s][j].wait_send()

    @pl.when(is_inner)
    def _():
        for s in range(nd):
            for j in range(2):
                ccp[s][j].wait_send()


def per_device(np_, nd, nt, x, g, w, c):
    T, D = x.shape[1:]
    K, C = w.shape[1:]
    KQ = K // nt
    o = nd - 1
    dma = pltpu.SemaphoreType.DMA
    scratch = [
        pltpu.VMEM((T, D), BF16),
        pltpu.VMEM((1, D), F32),
        pltpu.VMEM((K, C), BF16),
        pltpu.VMEM((T, C), BF16),
        pltpu.VMEM((T, 128), F32),
        pltpu.VMEM((o, T, 128), F32),
        pltpu.VMEM((o, T, K), BF16),
        pltpu.VMEM((nd, T, C), F32),
        pltpu.VMEM((o, T, C), BF16),
        pltpu.VMEM((o, T, C), BF16),
        pltpu.VMEM((T, C), BF16),
        pltpu.VMEM((T, C), BF16),
        pltpu.VMEM((o, T, C), BF16),
        pltpu.VMEM((nd, 4, T, KQ), BF16),
        pltpu.VMEM((nd, 4, T, KQ), BF16),
        dma((3,)), dma((NS,)),
        dma((o,)), dma((o,)), dma((o, NS)), dma((o, NS)), dma((o,)), dma((o,)),
        dma((o,)), dma((o,)), dma, dma,
        dma((nd,)), dma((nd,)), dma((nd, 2)), dma((nd, 2)), dma((nd, 2)), dma((nd,)),
    ]
    hbm = pl.BlockSpec(memory_space=pl.ANY)
    return pl.pallas_call(
        functools.partial(kernel, np_, nd, nt),
        out_shape=(
            jax.ShapeDtypeStruct((1, T, C), BF16),
            jax.ShapeDtypeStruct((1, T * nd, KQ), BF16),
        ),
        in_specs=[hbm] * 4,
        out_specs=(hbm, pl.BlockSpec(memory_space=pltpu.VMEM)),
        scratch_shapes=scratch,
        compiler_params=pltpu.CompilerParams(
            collective_id=0, has_side_effects=True, vmem_limit_bytes=58 * 2**20
        ),
        cost_estimate=pl.CostEstimate(
            flops=4 * T * nd * K * C, bytes_accessed=2 * K * C + 4 * T * D, transcendentals=T * C
        ),
    )(x, g, w, c)


def solution(mesh):
    in_specs = (
        P("pipe", "dp", None),
        P("pipe", None),
        P("pipe", "dp", "tensor"),
        P("pipe", "dp", "tensor"),
    )
    out_specs = (P("pipe", "dp", "tensor"), P("pipe", None, ("dp", "tensor")))
    body = functools.partial(per_device, mesh.shape["pipe"], mesh.shape["dp"], mesh.shape["tensor"])
    return jax.shard_map(body, mesh=mesh, in_specs=in_specs, out_specs=out_specs, check_vma=False)
```

```python
import functools

import jax
import jax.numpy as jnp
from jax import lax
from jax.experimental import pallas as pl
from jax.experimental.pallas import tpu as pltpu
from jax.sharding import PartitionSpec as P

F32 = jnp.float32
BF16 = jnp.bfloat16
MESH = pl.DeviceIdType.MESH
NB = 2
NS = 4


def kernel(
    np_, nd, nt,
    x_ref, g_ref, w_ref, c_ref,
    sh_ref, ng_ref,
    xv, gv, wv, cv, rs, rsr, xr, acc, ps, pr, lo, pgv, gp, rb,
    lsem, wsem,
    st_s, st_r, x_s, x_r, p_s, p_r, g_s, g_r, sh_s, sh_r,
    a_s, a_r, r_s, r_r, c_s, c_r,
):
    p = lax.axis_index("pipe")
    d = lax.axis_index("dp")
    t = lax.axis_index("tensor")
    T, D = x_ref.shape[1], x_ref.shape[2]
    K, C = w_ref.shape[1], w_ref.shape[2]
    KC, KQ, TB = K // NS, K // nt, T // NB

    def remote(src, dst, ss, rsem, **dev):
        return pltpu.make_async_remote_copy(
            src_ref=src, dst_ref=dst, send_sem=ss, recv_sem=rsem,
            device_id=dev, device_id_type=MESH,
        )

    nxt, prv = lax.rem(p + 1, np_), lax.rem(p + np_ - 1, np_)
    barrier = pltpu.get_barrier_semaphore()
    for o in range(1, nd):
        pl.semaphore_signal(barrier, inc=1, device_id={"dp": lax.rem(d + o, nd)}, device_id_type=MESH)
    for o in range(1, nt):
        pl.semaphore_signal(barrier, inc=1, device_id={"tensor": lax.rem(t + o, nt)}, device_id_type=MESH)
    pl.semaphore_signal(barrier, inc=1, device_id={"pipe": nxt}, device_id_type=MESH)
    pl.semaphore_signal(barrier, inc=1, device_id={"pipe": prv}, device_id_type=MESH)

    cx = pltpu.make_async_copy(x_ref.at[0], xv, lsem.at[0])
    cg = pltpu.make_async_copy(g_ref, gv, lsem.at[1])
    cc = pltpu.make_async_copy(c_ref.at[0], cv, lsem.at[2])
    cx.start()
    cg.start()
    cws = [
        pltpu.make_async_copy(w_ref.at[0, pl.ds(k * KC, KC)], wv.at[pl.ds(k * KC, KC)], wsem.at[k])
        for k in range(NS)
    ]
    for cw in cws:
        cw.start()
    cc.start()

    def peer(o):
        return lax.rem(d + o, nd)

    xcp = [[[
        remote(
            x_ref.at[0, pl.ds(b * TB, TB), pl.ds(pl.multiple_of(peer(o) * K + k * KC, 128), KC)],
            xr.at[o - 1, pl.ds(b * TB, TB), pl.ds(k * KC, KC)],
            x_s.at[b, o - 1, k], x_r.at[b, o - 1, k], dp=peer(o),
        ) for o in range(1, nd)] for k in range(NS)] for b in range(NB)]
    stcp = [
        remote(rs, rsr.at[o - 1], st_s.at[o - 1], st_r.at[o - 1], dp=peer(o)) for o in range(1, nd)
    ]
    pcp = [[
        remote(
            ps.at[b, nd - o - 1], pr.at[b, o - 1], p_s.at[b, o - 1], p_r.at[b, o - 1], dp=peer(o)
        ) for o in range(1, nd)] for b in range(NB)]
    gcp = [[
        remote(
            pgv.at[b, 0], pgv.at[b, o], g_s.at[b, o - 1], g_r.at[b, o - 1], dp=peer(o)
        ) for o in range(1, nd)] for b in range(NB)]
    shcp = [
        remote(lo.at[b], sh_ref.at[0, pl.ds(b * TB, TB)], sh_s.at[b], sh_r.at[b], pipe=nxt)
        for b in range(NB)
    ]

    def start_x(b, ks):
        for k in ks:
            for cp in xcp[b][k]:
                cp.start()

    pl.semaphore_wait(barrier, (nd - 1) + (nt - 1) + 2)

    start_x(0, range(NS))

    cx.wait()
    ss = jnp.zeros((T, 1), F32)
    SC = D // 8
    for k in range(8):
        xf = xv[:, k * SC:(k + 1) * SC].astype(F32)
        ss = ss + jnp.sum(xf * xf, axis=-1, keepdims=True)
    scale = lax.rsqrt(ss * (1.0 / D) + 1e-05)
    rs[...] = jnp.broadcast_to(scale, rs.shape)
    for cp in stcp:
        cp.start()
    start_x(1, range(1))

    cg.wait()

    def gain(k):
        return gv[:, pl.ds(pl.multiple_of(d * K + k * KC, 128), KC)]

    for k in range(NS):
        xf = xv[:, pl.ds(pl.multiple_of(d * K + k * KC, 128), KC)].astype(F32)
        nb = (xf * rs[:, 0:1] * gain(k)).astype(BF16)
        cws[k].wait()
        part = jnp.dot(nb, wv[k * KC:(k + 1) * KC, :], preferred_element_type=F32)
        if k == 0:
            acc[0] = part
        else:
            acc[0] += part
    for cp in stcp:
        cp.wait_recv()
    cc.wait()

    def project_peers(b):
        rows = slice(b * TB, (b + 1) * TB)
        for k in range(NS):
            for o in range(1, nd):
                xcp[b][k][o - 1].wait_recv()
                xf = xr[o - 1, rows, k * KC:(k + 1) * KC].astype(F32)
                nb = (xf * rsr[o - 1, rows, 0:1] * gain(k)).astype(BF16)
                part = jnp.dot(nb, wv[k * KC:(k + 1) * KC, :], preferred_element_type=F32)
                if k == 0:
                    acc[o, rows] = part
                elif k < NS - 1:
                    acc[o, rows] += part
                else:
                    ps[b, o - 1] = (acc[o, rows] + part).astype(BF16)
                    pcp[b][nd - o - 1].start()

    k0 = 0.7978845608028654
    k1 = 0.044715
    CB = 256

    def activate(b):
        rows = slice(b * TB, (b + 1) * TB)
        for cp in pcp[b]:
            cp.wait_recv()
        for i in range(C // CB):
            cols = slice(i * CB, (i + 1) * CB)
            pre = acc[0, rows, cols].astype(BF16).astype(F32)
            for o in range(1, nd):
                pre = pre + pr[b, o - 1, :, cols].astype(F32)
            sq = pre * pre
            th = jnp.tanh(k0 * (pre + k1 * (sq * pre)))
            cdf = 0.5 * (1.0 + th)
            slope = cdf + 0.5 * pre * ((1.0 - th * th) * (k0 * (1.0 + 3.0 * k1 * sq)))
            pgv[b, 0, :, cols] = (cv[rows, cols].astype(F32) * slope).astype(BF16)
            res = xv[rows, pl.ds(pl.multiple_of(t * C + i * CB, 128), CB)].astype(F32)
            lo[b, :, cols] = (res + pre * cdf).astype(BF16)
        for cp in gcp[b]:
            cp.start()
        shcp[b].start()

    low = t < 2
    inner = jnp.where(low, 1, 2)
    outer = jnp.where(low, 0, 3)
    is_outer = t == outer
    is_inner = t == inner
    partner = inner + outer - t
    dests = [3 - outer, 3 - inner, partner, t]
    acp, rcp, ccp = [], [], []
    for s in range(NB):
        acp.append(remote(gp.at[s, 2], rb.at[s, 0], a_s.at[s], a_r.at[s], tensor=partner))
        rcp.append([remote(gp.at[s, j], rb.at[s, 2 + j], r_s.at[s, j], r_r.at[s, j], tensor=partner) for j in range(2)])
        ccp.append([remote(gp.at[s, j], rb.at[s, 1], c_s.at[s, j], c_r.at[s], tensor=dests[j]) for j in range(2)])

    def input_grad(b):
        for cp in gcp[b]:
            cp.wait_recv()
        for j in range(4):
            pg = pgv[b].reshape(nd * TB, C)
            wb = wv[pl.ds(pl.multiple_of(dests[j] * KQ, KQ), KQ), :]
            part = lax.dot_general(pg, wb, (((1,), (1,)), ((), ())), preferred_element_type=F32)
            gp[b, j] = part.astype(BF16)
            if j < 2:
                @pl.when(is_outer)
                def _():
                    rcp[b][j].start()
            elif j == 2:
                acp[b].start()

    def relay(b, j):
        @pl.when(is_inner)
        def _():
            rcp[b][j].wait_recv()
            gp[b, j] = (gp[b, j].astype(F32) + rb[b, 2 + j].astype(F32)).astype(BF16)
            ccp[b][j].start()

    def finish(b):
        acp[b].wait_recv()
        ccp[b][0].wait_recv()
        for o in range(nd):
            r = slice(o * TB, (o + 1) * TB)
            row = pl.multiple_of(lax.rem(d - o + nd, nd) * T + b * TB, TB)
            ng_ref[0, pl.ds(row, TB), :] = (
                gp[b, 3, r].astype(F32) + rb[b, 0, r].astype(F32) + rb[b, 1, r].astype(F32)
            ).astype(BF16)

    project_peers(0)
    start_x(1, range(1, 3))
    activate(0)
    start_x(1, range(3, NS))
    input_grad(0)
    project_peers(1)
    relay(0, 0)
    activate(1)
    relay(0, 1)
    input_grad(1)
    relay(1, 0)
    relay(1, 1)
    finish(0)
    finish(1)

    for b in range(NB):
        for k in range(NS):
            for cp in xcp[b][k]:
                cp.wait_send()
        for cp in pcp[b] + gcp[b]:
            cp.wait_send()
        acp[b].wait_send()
        shcp[b].wait()
    for cp in stcp:
        cp.wait_send()

    @pl.when(is_outer)
    def _():
        for s in range(NB):
            for j in range(2):
                rcp[s][j].wait_send()

    @pl.when(is_inner)
    def _():
        for s in range(NB):
            for j in range(2):
                ccp[s][j].wait_send()


def place(a_ref, b_ref, oa_ref, ob_ref, sem):
    one = pltpu.make_async_copy(a_ref, oa_ref, sem.at[0])
    two = pltpu.make_async_copy(b_ref, ob_ref, sem.at[1])
    one.start()
    two.start()
    one.wait()
    two.wait()


def per_device(np_, nd, nt, x, g, w, c):
    T, D = x.shape[1:]
    K, C = w.shape[1:]
    KQ, TB = K // nt, T // NB
    o = nd - 1
    dma = pltpu.SemaphoreType.DMA
    scratch = [
        pltpu.VMEM((T, D), BF16),
        pltpu.VMEM((1, D), F32),
        pltpu.VMEM((K, C), BF16),
        pltpu.VMEM((T, C), BF16),
        pltpu.VMEM((T, 128), F32),
        pltpu.VMEM((o, T, 128), F32),
        pltpu.VMEM((o, T, K), BF16),
        pltpu.VMEM((nd, T, C), F32),
        pltpu.VMEM((NB, o, TB, C), BF16),
        pltpu.VMEM((NB, o, TB, C), BF16),
        pltpu.VMEM((NB, TB, C), BF16),
        pltpu.VMEM((NB, nd, TB, C), BF16),
        pltpu.VMEM((NB, 4, nd * TB, KQ), BF16),
        pltpu.VMEM((NB, 4, nd * TB, KQ), BF16),
        dma((3,)), dma((NS,)),
        dma((o,)), dma((o,)), dma((NB, o, NS)), dma((NB, o, NS)), dma((NB, o)), dma((NB, o)),
        dma((NB, o)), dma((NB, o)), dma((NB,)), dma((NB,)),
        dma((NB,)), dma((NB,)), dma((NB, 2)), dma((NB, 2)), dma((NB, 2)), dma((NB,)),
    ]
    hbm = pl.BlockSpec(memory_space=pl.ANY)
    shifted, grad = pl.pallas_call(
        functools.partial(kernel, np_, nd, nt),
        out_shape=(
            jax.ShapeDtypeStruct((1, T, C), BF16),
            jax.ShapeDtypeStruct((1, T * nd, KQ), BF16),
        ),
        in_specs=[hbm] * 4,
        out_specs=(hbm, pl.BlockSpec(memory_space=pltpu.VMEM)),
        scratch_shapes=scratch,
        compiler_params=pltpu.CompilerParams(
            collective_id=0, has_side_effects=True, vmem_limit_bytes=58 * 2**20
        ),
        cost_estimate=pl.CostEstimate(
            flops=4 * T * nd * K * C, bytes_accessed=2 * K * C + 4 * T * D, transcendentals=T * C
        ),
    )(x, g, w, c)
    return pl.pallas_call(
        place,
        out_shape=(
            jax.ShapeDtypeStruct(shifted.shape, BF16),
            jax.ShapeDtypeStruct(grad.shape, BF16),
        ),
        in_specs=[hbm] * 2,
        out_specs=(hbm, hbm),
        scratch_shapes=[dma((2,))],
    )(shifted, grad)


def solution(mesh):
    in_specs = (
        P("pipe", "dp", None),
        P("pipe", None),
        P("pipe", "dp", "tensor"),
        P("pipe", "dp", "tensor"),
    )
    out_specs = (P("pipe", "dp", "tensor"), P("pipe", None, ("dp", "tensor")))
    body = functools.partial(per_device, mesh.shape["pipe"], mesh.shape["dp"], mesh.shape["tensor"])
    return jax.shard_map(body, mesh=mesh, in_specs=in_specs, out_specs=out_specs, check_vma=False)
```

```python
import functools

import jax
import jax.numpy as jnp
from jax import lax
from jax.experimental import pallas as pl
from jax.experimental.pallas import tpu as pltpu
from jax.sharding import PartitionSpec as P

F32 = jnp.float32
BF16 = jnp.bfloat16
MESH = pl.DeviceIdType.MESH
NB = 2
NS = 4


def kernel(
    np_, nd, nt,
    x_ref, g_ref, w_ref, c_ref,
    sh_ref, ng_ref,
    xv, gv, wv, cv, rs, rsr, xr, acc, ps, pr, lo, pgv, gp, rb,
    lsem, wsem,
    st_s, st_r, x_s, x_r, p_s, p_r, g_s, g_r, sh_s, sh_r,
    a_s, a_r, r_s, r_r, c_s, c_r,
):
    p = lax.axis_index("pipe")
    d = lax.axis_index("dp")
    t = lax.axis_index("tensor")
    T, D = x_ref.shape[1], x_ref.shape[2]
    K, C = w_ref.shape[1], w_ref.shape[2]
    KC, KQ, TB = K // NS, K // nt, T // NB

    def remote(src, dst, ss, rsem, **dev):
        return pltpu.make_async_remote_copy(
            src_ref=src, dst_ref=dst, send_sem=ss, recv_sem=rsem,
            device_id=dev, device_id_type=MESH,
        )

    nxt, prv = lax.rem(p + 1, np_), lax.rem(p + np_ - 1, np_)
    barrier = pltpu.get_barrier_semaphore()
    for o in range(1, nd):
        pl.semaphore_signal(barrier, inc=1, device_id={"dp": lax.rem(d + o, nd)}, device_id_type=MESH)
    for o in range(1, nt):
        pl.semaphore_signal(barrier, inc=1, device_id={"tensor": lax.rem(t + o, nt)}, device_id_type=MESH)
    pl.semaphore_signal(barrier, inc=1, device_id={"pipe": nxt}, device_id_type=MESH)
    pl.semaphore_signal(barrier, inc=1, device_id={"pipe": prv}, device_id_type=MESH)

    cx = pltpu.make_async_copy(x_ref.at[0], xv, lsem.at[0])
    cg = pltpu.make_async_copy(g_ref, gv, lsem.at[1])
    cc = pltpu.make_async_copy(c_ref.at[0], cv, lsem.at[2])
    cx.start()
    cg.start()
    cws = [
        pltpu.make_async_copy(w_ref.at[0, pl.ds(k * KC, KC)], wv.at[pl.ds(k * KC, KC)], wsem.at[k])
        for k in range(NS)
    ]
    for cw in cws:
        cw.start()
    cc.start()

    def peer(o):
        return lax.rem(d + o, nd)

    xcp = [[[
        remote(
            x_ref.at[0, pl.ds(b * TB, TB), pl.ds(pl.multiple_of(peer(o) * K + k * KC, 128), KC)],
            xr.at[o - 1, pl.ds(b * TB, TB), pl.ds(k * KC, KC)],
            x_s.at[b, o - 1, k], x_r.at[b, o - 1, k], dp=peer(o),
        ) for o in range(1, nd)] for k in range(NS)] for b in range(NB)]
    stcp = [
        remote(rs, rsr.at[o - 1], st_s.at[o - 1], st_r.at[o - 1], dp=peer(o)) for o in range(1, nd)
    ]
    pcp = [[
        remote(
            ps.at[b, nd - o - 1], pr.at[b, o - 1], p_s.at[b, o - 1], p_r.at[b, o - 1], dp=peer(o)
        ) for o in range(1, nd)] for b in range(NB)]
    gcp = [[
        remote(
            pgv.at[b, 0], pgv.at[b, o], g_s.at[b, o - 1], g_r.at[b, o - 1], dp=peer(o)
        ) for o in range(1, nd)] for b in range(NB)]
    shcp = [
        remote(lo.at[b], sh_ref.at[0, pl.ds(b * TB, TB)], sh_s.at[b], sh_r.at[b], pipe=nxt)
        for b in range(NB)
    ]

    def start_x(b, ks):
        for k in ks:
            for cp in xcp[b][k]:
                cp.start()

    pl.semaphore_wait(barrier, (nd - 1) + (nt - 1) + 2)

    start_x(0, range(NS))

    cx.wait()
    ss = jnp.zeros((T, 1), F32)
    SC = D // 8
    for k in range(8):
        xf = xv[:, k * SC:(k + 1) * SC].astype(F32)
        ss = ss + jnp.sum(xf * xf, axis=-1, keepdims=True)
    scale = lax.rsqrt(ss * (1.0 / D) + 1e-05)
    rs[...] = jnp.broadcast_to(scale, rs.shape)
    for cp in stcp:
        cp.start()
    start_x(1, range(2))

    cg.wait()

    def gain(k):
        return gv[:, pl.ds(pl.multiple_of(d * K + k * KC, 128), KC)]

    for k in range(NS):
        xf = xv[:, pl.ds(pl.multiple_of(d * K + k * KC, 128), KC)].astype(F32)
        nb = (xf * rs[:, 0:1] * gain(k)).astype(BF16)
        cws[k].wait()
        part = jnp.dot(nb, wv[k * KC:(k + 1) * KC, :], preferred_element_type=F32)
        if k == 0:
            acc[0] = part
        else:
            acc[0] += part
    for cp in stcp:
        cp.wait_recv()
    cc.wait()

    def project_peers(b):
        rows = slice(b * TB, (b + 1) * TB)
        for k in range(NS):
            for o in range(1, nd):
                xcp[b][k][o - 1].wait_recv()
                xf = xr[o - 1, rows, k * KC:(k + 1) * KC].astype(F32)
                nb = (xf * rsr[o - 1, rows, 0:1] * gain(k)).astype(BF16)
                part = jnp.dot(nb, wv[k * KC:(k + 1) * KC, :], preferred_element_type=F32)
                if k == 0:
                    acc[o, rows] = part
                elif k < NS - 1:
                    acc[o, rows] += part
                else:
                    ps[b, o - 1] = (acc[o, rows] + part).astype(BF16)
                    pcp[b][nd - o - 1].start()

    k0 = 0.7978845608028654
    k1 = 0.044715
    CB = 256

    def activate(b):
        rows = slice(b * TB, (b + 1) * TB)
        for cp in pcp[b]:
            cp.wait_recv()
        for i in range(C // CB):
            cols = slice(i * CB, (i + 1) * CB)
            pre = acc[0, rows, cols].astype(BF16).astype(F32)
            for o in range(1, nd):
                pre = pre + pr[b, o - 1, :, cols].astype(F32)
            sq = pre * pre
            th = jnp.tanh(k0 * (pre + k1 * (sq * pre)))
            cdf = 0.5 * (1.0 + th)
            slope = cdf + 0.5 * pre * ((1.0 - th * th) * (k0 * (1.0 + 3.0 * k1 * sq)))
            pgv[b, 0, :, cols] = (cv[rows, cols].astype(F32) * slope).astype(BF16)
            res = xv[rows, pl.ds(pl.multiple_of(t * C + i * CB, 128), CB)].astype(F32)
            lo[b, :, cols] = (res + pre * cdf).astype(BF16)
        for cp in gcp[b]:
            cp.start()
        shcp[b].start()

    low = t < 2
    inner = jnp.where(low, 1, 2)
    outer = jnp.where(low, 0, 3)
    is_outer = t == outer
    is_inner = t == inner
    partner = inner + outer - t
    dests = [3 - outer, 3 - inner, partner, t]
    acp, rcp, ccp = [], [], []
    for s in range(NB):
        acp.append(remote(gp.at[s, 2], rb.at[s, 0], a_s.at[s], a_r.at[s], tensor=partner))
        rcp.append([remote(gp.at[s, j], rb.at[s, 2 + j], r_s.at[s, j], r_r.at[s, j], tensor=partner) for j in range(2)])
        ccp.append([remote(gp.at[s, j], rb.at[s, 1], c_s.at[s, j], c_r.at[s], tensor=dests[j]) for j in range(2)])

    def input_grad(b):
        for cp in gcp[b]:
            cp.wait_recv()
        for j in range(4):
            pg = pgv[b].reshape(nd * TB, C)
            wb = wv[pl.ds(pl.multiple_of(dests[j] * KQ, KQ), KQ), :]
            part = lax.dot_general(pg, wb, (((1,), (1,)), ((), ())), preferred_element_type=F32)
            gp[b, j] = part.astype(BF16)
            if j < 2:
                @pl.when(is_outer)
                def _():
                    rcp[b][j].start()
            elif j == 2:
                acp[b].start()

    def relay(b, j):
        @pl.when(is_inner)
        def _():
            rcp[b][j].wait_recv()
            gp[b, j] = (gp[b, j].astype(F32) + rb[b, 2 + j].astype(F32)).astype(BF16)
            ccp[b][j].start()

    def finish(b):
        acp[b].wait_recv()
        ccp[b][0].wait_recv()
        for o in range(nd):
            r = slice(o * TB, (o + 1) * TB)
            row = pl.multiple_of(lax.rem(d - o + nd, nd) * T + b * TB, TB)
            ng_ref[0, pl.ds(row, TB), :] = (
                gp[b, 3, r].astype(F32) + rb[b, 0, r].astype(F32) + rb[b, 1, r].astype(F32)
            ).astype(BF16)

    project_peers(0)
    start_x(1, range(2, NS))
    activate(0)
    project_peers(1)
    input_grad(0)
    activate(1)
    relay(0, 0)
    relay(0, 1)
    input_grad(1)
    relay(1, 0)
    relay(1, 1)
    finish(0)
    finish(1)

    for b in range(NB):
        for k in range(NS):
            for cp in xcp[b][k]:
                cp.wait_send()
        for cp in pcp[b] + gcp[b]:
            cp.wait_send()
        acp[b].wait_send()
        shcp[b].wait()
    for cp in stcp:
        cp.wait_send()

    @pl.when(is_outer)
    def _():
        for s in range(NB):
            for j in range(2):
                rcp[s][j].wait_send()

    @pl.when(is_inner)
    def _():
        for s in range(NB):
            for j in range(2):
                ccp[s][j].wait_send()


def place(a_ref, b_ref, oa_ref, ob_ref):
    oa_ref[...] = a_ref[...]
    ob_ref[...] = b_ref[...]


def per_device(np_, nd, nt, x, g, w, c):
    T, D = x.shape[1:]
    K, C = w.shape[1:]
    KQ, TB = K // nt, T // NB
    o = nd - 1
    dma = pltpu.SemaphoreType.DMA
    scratch = [
        pltpu.VMEM((T, D), BF16),
        pltpu.VMEM((1, D), F32),
        pltpu.VMEM((K, C), BF16),
        pltpu.VMEM((T, C), BF16),
        pltpu.VMEM((T, 128), F32),
        pltpu.VMEM((o, T, 128), F32),
        pltpu.VMEM((o, T, K), BF16),
        pltpu.VMEM((nd, T, C), F32),
        pltpu.VMEM((NB, o, TB, C), BF16),
        pltpu.VMEM((NB, o, TB, C), BF16),
        pltpu.VMEM((NB, TB, C), BF16),
        pltpu.VMEM((NB, nd, TB, C), BF16),
        pltpu.VMEM((NB, 4, nd * TB, KQ), BF16),
        pltpu.VMEM((NB, 4, nd * TB, KQ), BF16),
        dma((3,)), dma((NS,)),
        dma((o,)), dma((o,)), dma((NB, o, NS)), dma((NB, o, NS)), dma((NB, o)), dma((NB, o)),
        dma((NB, o)), dma((NB, o)), dma((NB,)), dma((NB,)),
        dma((NB,)), dma((NB,)), dma((NB, 2)), dma((NB, 2)), dma((NB, 2)), dma((NB,)),
    ]
    vmem = pl.BlockSpec(memory_space=pltpu.VMEM)
    hbm = pl.BlockSpec(memory_space=pl.ANY)
    shifted, grad = pl.pallas_call(
        functools.partial(kernel, np_, nd, nt),
        out_shape=(
            jax.ShapeDtypeStruct((1, T, C), BF16),
            jax.ShapeDtypeStruct((1, T * nd, KQ), BF16),
        ),
        in_specs=[hbm] * 4,
        out_specs=(hbm, pl.BlockSpec(memory_space=pltpu.VMEM)),
        scratch_shapes=scratch,
        compiler_params=pltpu.CompilerParams(
            collective_id=0, has_side_effects=True, vmem_limit_bytes=58 * 2**20
        ),
        cost_estimate=pl.CostEstimate(
            flops=4 * T * nd * K * C, bytes_accessed=2 * K * C + 4 * T * D, transcendentals=T * C
        ),
    )(x, g, w, c)
    return pl.pallas_call(
        place,
        out_shape=(
            jax.ShapeDtypeStruct(shifted.shape, BF16),
            jax.ShapeDtypeStruct(grad.shape, BF16),
        ),
        in_specs=[vmem] * 2,
        out_specs=(vmem, vmem),
    )(shifted, grad)


def solution(mesh):
    in_specs = (
        P("pipe", "dp", None),
        P("pipe", None),
        P("pipe", "dp", "tensor"),
        P("pipe", "dp", "tensor"),
    )
    out_specs = (P("pipe", "dp", "tensor"), P("pipe", None, ("dp", "tensor")))
    body = functools.partial(per_device, mesh.shape["pipe"], mesh.shape["dp"], mesh.shape["tensor"])
    return jax.shard_map(body, mesh=mesh, in_specs=in_specs, out_specs=out_specs, check_vma=False)
```

```python
import functools

import jax
import jax.numpy as jnp
from jax import lax
from jax.experimental import pallas as pl
from jax.experimental.pallas import tpu as pltpu
from jax.sharding import PartitionSpec as P

F32 = jnp.float32
BF16 = jnp.bfloat16
MESH = pl.DeviceIdType.MESH
NB = 2
NS = 4


def kernel(
    np_, nd, nt,
    x_ref, g_ref, w_ref, c_ref,
    sh_ref, ng_ref,
    xv, gv, wv, cv, rs, rsr, xr, acc, ps, pr, lo, pgv, gp, rb,
    lsem, wsem,
    st_s, st_r, x_s, x_r, p_s, p_r, g_s, g_r, sh_s, sh_r,
    a_s, a_r, r_s, r_r, c_s, c_r,
):
    p = lax.axis_index("pipe")
    d = lax.axis_index("dp")
    t = lax.axis_index("tensor")
    T, D = x_ref.shape[1], x_ref.shape[2]
    K, C = w_ref.shape[1], w_ref.shape[2]
    KC, KQ, TB = K // NS, K // nt, T // NB

    def remote(src, dst, ss, rsem, **dev):
        return pltpu.make_async_remote_copy(
            src_ref=src, dst_ref=dst, send_sem=ss, recv_sem=rsem,
            device_id=dev, device_id_type=MESH,
        )

    nxt, prv = lax.rem(p + 1, np_), lax.rem(p + np_ - 1, np_)
    barrier = pltpu.get_barrier_semaphore()
    for o in range(1, nd):
        pl.semaphore_signal(barrier, inc=1, device_id={"dp": lax.rem(d + o, nd)}, device_id_type=MESH)
    for o in range(1, nt):
        pl.semaphore_signal(barrier, inc=1, device_id={"tensor": lax.rem(t + o, nt)}, device_id_type=MESH)
    pl.semaphore_signal(barrier, inc=1, device_id={"pipe": nxt}, device_id_type=MESH)
    pl.semaphore_signal(barrier, inc=1, device_id={"pipe": prv}, device_id_type=MESH)

    cx = pltpu.make_async_copy(x_ref.at[0], xv, lsem.at[0])
    cg = pltpu.make_async_copy(g_ref, gv, lsem.at[1])
    cc = pltpu.make_async_copy(c_ref.at[0], cv, lsem.at[2])
    cx.start()
    cg.start()
    cws = [
        pltpu.make_async_copy(w_ref.at[0, pl.ds(k * KC, KC)], wv.at[pl.ds(k * KC, KC)], wsem.at[k])
        for k in range(NS)
    ]
    for cw in cws:
        cw.start()
    cc.start()

    def peer(o):
        return lax.rem(d + o, nd)

    xcp = [[[
        remote(
            xv.at[pl.ds(b * TB, TB), pl.ds(pl.multiple_of(peer(o) * K + k * KC, 128), KC)],
            xr.at[o - 1, pl.ds(b * TB, TB), pl.ds(k * KC, KC)],
            x_s.at[b, o - 1, k], x_r.at[b, o - 1, k], dp=peer(o),
        ) for o in range(1, nd)] for k in range(NS)] for b in range(NB)]
    stcp = [
        remote(rs, rsr.at[o - 1], st_s.at[o - 1], st_r.at[o - 1], dp=peer(o)) for o in range(1, nd)
    ]
    pcp = [[
        remote(
            ps.at[b, nd - o - 1], pr.at[b, o - 1], p_s.at[b, o - 1], p_r.at[b, o - 1], dp=peer(o)
        ) for o in range(1, nd)] for b in range(NB)]
    gcp = [[
        remote(
            pgv.at[b, 0], pgv.at[b, o], g_s.at[b, o - 1], g_r.at[b, o - 1], dp=peer(o)
        ) for o in range(1, nd)] for b in range(NB)]
    shcp = [
        remote(lo.at[b], sh_ref.at[0, pl.ds(b * TB, TB)], sh_s.at[b], sh_r.at[b], pipe=nxt)
        for b in range(NB)
    ]

    def start_x(b, ks):
        for k in ks:
            for cp in xcp[b][k]:
                cp.start()

    cx.wait()
    ss = jnp.zeros((T, 1), F32)
    SC = D // 8
    for k in range(8):
        xf = xv[:, k * SC:(k + 1) * SC].astype(F32)
        ss = ss + jnp.sum(xf * xf, axis=-1, keepdims=True)
    scale = lax.rsqrt(ss * (1.0 / D) + 1e-05)
    rs[...] = jnp.broadcast_to(scale, rs.shape)

    pl.semaphore_wait(barrier, (nd - 1) + (nt - 1) + 2)

    start_x(0, range(NS))
    for cp in stcp:
        cp.start()
    start_x(1, range(2))

    cg.wait()

    def gain(k):
        return gv[:, pl.ds(pl.multiple_of(d * K + k * KC, 128), KC)]

    for k in range(NS):
        xf = xv[:, pl.ds(pl.multiple_of(d * K + k * KC, 128), KC)].astype(F32)
        nb = (xf * rs[:, 0:1] * gain(k)).astype(BF16)
        cws[k].wait()
        part = jnp.dot(nb, wv[k * KC:(k + 1) * KC, :], preferred_element_type=F32)
        if k == 0:
            acc[0] = part
        else:
            acc[0] += part
    for cp in stcp:
        cp.wait_recv()
    cc.wait()

    def project_peers(b):
        rows = slice(b * TB, (b + 1) * TB)
        for k in range(NS):
            for o in range(1, nd):
                xcp[b][k][o - 1].wait_recv()
                xf = xr[o - 1, rows, k * KC:(k + 1) * KC].astype(F32)
                nb = (xf * rsr[o - 1, rows, 0:1] * gain(k)).astype(BF16)
                part = jnp.dot(nb, wv[k * KC:(k + 1) * KC, :], preferred_element_type=F32)
                if k == 0:
                    acc[o, rows] = part
                elif k < NS - 1:
                    acc[o, rows] += part
                else:
                    ps[b, o - 1] = (acc[o, rows] + part).astype(BF16)
                    pcp[b][nd - o - 1].start()

    k0 = 0.7978845608028654
    k1 = 0.044715
    CB = 256

    def activate(b):
        rows = slice(b * TB, (b + 1) * TB)
        for cp in pcp[b]:
            cp.wait_recv()
        for i in range(C // CB):
            cols = slice(i * CB, (i + 1) * CB)
            pre = acc[0, rows, cols].astype(BF16).astype(F32)
            for o in range(1, nd):
                pre = pre + pr[b, o - 1, :, cols].astype(F32)
            sq = pre * pre
            th = jnp.tanh(k0 * (pre + k1 * (sq * pre)))
            cdf = 0.5 * (1.0 + th)
            slope = cdf + 0.5 * pre * ((1.0 - th * th) * (k0 * (1.0 + 3.0 * k1 * sq)))
            pgv[b, 0, :, cols] = (cv[rows, cols].astype(F32) * slope).astype(BF16)
            res = xv[rows, pl.ds(pl.multiple_of(t * C + i * CB, 128), CB)].astype(F32)
            lo[b, :, cols] = (res + pre * cdf).astype(BF16)
        for cp in gcp[b]:
            cp.start()
        shcp[b].start()

    low = t < 2
    inner = jnp.where(low, 1, 2)
    outer = jnp.where(low, 0, 3)
    is_outer = t == outer
    is_inner = t == inner
    partner = inner + outer - t
    dests = [3 - outer, 3 - inner, partner, t]
    acp, rcp, ccp = [], [], []
    for s in range(NB):
        acp.append(remote(gp.at[s, 2], rb.at[s, 0], a_s.at[s], a_r.at[s], tensor=partner))
        rcp.append([remote(gp.at[s, j], rb.at[s, 2 + j], r_s.at[s, j], r_r.at[s, j], tensor=partner) for j in range(2)])
        ccp.append([remote(gp.at[s, j], rb.at[s, 1], c_s.at[s, j], c_r.at[s], tensor=dests[j]) for j in range(2)])

    def input_grad(b):
        for cp in gcp[b]:
            cp.wait_recv()
        for j in range(4):
            pg = pgv[b].reshape(nd * TB, C)
            wb = wv[pl.ds(pl.multiple_of(dests[j] * KQ, KQ), KQ), :]
            part = lax.dot_general(pg, wb, (((1,), (1,)), ((), ())), preferred_element_type=F32)
            gp[b, j] = part.astype(BF16)
            if j < 2:
                @pl.when(is_outer)
                def _():
                    rcp[b][j].start()
            elif j == 2:
                acp[b].start()

    def relay(b, j):
        @pl.when(is_inner)
        def _():
            rcp[b][j].wait_recv()
            gp[b, j] = (gp[b, j].astype(F32) + rb[b, 2 + j].astype(F32)).astype(BF16)
            ccp[b][j].start()

    def finish(b):
        acp[b].wait_recv()
        ccp[b][0].wait_recv()
        for o in range(nd):
            r = slice(o * TB, (o + 1) * TB)
            row = pl.multiple_of(lax.rem(d - o + nd, nd) * T + b * TB, TB)
            ng_ref[0, pl.ds(row, TB), :] = (
                gp[b, 3, r].astype(F32) + rb[b, 0, r].astype(F32) + rb[b, 1, r].astype(F32)
            ).astype(BF16)

    project_peers(0)
    start_x(1, range(2, NS))
    activate(0)
    project_peers(1)
    input_grad(0)
    activate(1)
    relay(0, 0)
    relay(0, 1)
    input_grad(1)
    relay(1, 0)
    relay(1, 1)
    finish(0)
    finish(1)

    for b in range(NB):
        for k in range(NS):
            for cp in xcp[b][k]:
                cp.wait_send()
        for cp in pcp[b] + gcp[b]:
            cp.wait_send()
        acp[b].wait_send()
        shcp[b].wait()
    for cp in stcp:
        cp.wait_send()

    @pl.when(is_outer)
    def _():
        for s in range(NB):
            for j in range(2):
                rcp[s][j].wait_send()

    @pl.when(is_inner)
    def _():
        for s in range(NB):
            for j in range(2):
                ccp[s][j].wait_send()


def place(a_ref, b_ref, oa_ref, ob_ref):
    oa_ref[...] = a_ref[...]
    ob_ref[...] = b_ref[...]


def per_device(np_, nd, nt, x, g, w, c):
    T, D = x.shape[1:]
    K, C = w.shape[1:]
    KQ, TB = K // nt, T // NB
    o = nd - 1
    dma = pltpu.SemaphoreType.DMA
    scratch = [
        pltpu.VMEM((T, D), BF16),
        pltpu.VMEM((1, D), F32),
        pltpu.VMEM((K, C), BF16),
        pltpu.VMEM((T, C), BF16),
        pltpu.VMEM((T, 128), F32),
        pltpu.VMEM((o, T, 128), F32),
        pltpu.VMEM((o, T, K), BF16),
        pltpu.VMEM((nd, T, C), F32),
        pltpu.VMEM((NB, o, TB, C), BF16),
        pltpu.VMEM((NB, o, TB, C), BF16),
        pltpu.VMEM((NB, TB, C), BF16),
        pltpu.VMEM((NB, nd, TB, C), BF16),
        pltpu.VMEM((NB, 4, nd * TB, KQ), BF16),
        pltpu.VMEM((NB, 4, nd * TB, KQ), BF16),
        dma((3,)), dma((NS,)),
        dma((o,)), dma((o,)), dma((NB, o, NS)), dma((NB, o, NS)), dma((NB, o)), dma((NB, o)),
        dma((NB, o)), dma((NB, o)), dma((NB,)), dma((NB,)),
        dma((NB,)), dma((NB,)), dma((NB, 2)), dma((NB, 2)), dma((NB, 2)), dma((NB,)),
    ]
    vmem = pl.BlockSpec(memory_space=pltpu.VMEM)
    hbm = pl.BlockSpec(memory_space=pl.ANY)
    shifted, grad = pl.pallas_call(
        functools.partial(kernel, np_, nd, nt),
        out_shape=(
            jax.ShapeDtypeStruct((1, T, C), BF16),
            jax.ShapeDtypeStruct((1, T * nd, KQ), BF16),
        ),
        in_specs=[hbm] * 4,
        out_specs=(hbm, pl.BlockSpec(memory_space=pltpu.VMEM)),
        scratch_shapes=scratch,
        compiler_params=pltpu.CompilerParams(
            collective_id=0, has_side_effects=True, vmem_limit_bytes=58 * 2**20
        ),
        cost_estimate=pl.CostEstimate(
            flops=4 * T * nd * K * C, bytes_accessed=2 * K * C + 4 * T * D, transcendentals=T * C
        ),
    )(x, g, w, c)
    return pl.pallas_call(
        place,
        out_shape=(
            jax.ShapeDtypeStruct(shifted.shape, BF16),
            jax.ShapeDtypeStruct(grad.shape, BF16),
        ),
        in_specs=[vmem] * 2,
        out_specs=(vmem, vmem),
    )(shifted, grad)


def solution(mesh):
    in_specs = (
        P("pipe", "dp", None),
        P("pipe", None),
        P("pipe", "dp", "tensor"),
        P("pipe", "dp", "tensor"),
    )
    out_specs = (P("pipe", "dp", "tensor"), P("pipe", None, ("dp", "tensor")))
    body = functools.partial(per_device, mesh.shape["pipe"], mesh.shape["dp"], mesh.shape["tensor"])
    return jax.shard_map(body, mesh=mesh, in_specs=in_specs, out_specs=out_specs, check_vma=False)
```

```python
import functools

import jax
import jax.numpy as jnp
from jax import lax
from jax.experimental import pallas as pl
from jax.experimental.pallas import tpu as pltpu
from jax.sharding import PartitionSpec as P

F32 = jnp.float32
BF16 = jnp.bfloat16
MESH = pl.DeviceIdType.MESH
NB = 2
NS = 4


def kernel(
    np_, nd, nt,
    x_ref, g_ref, w_ref, c_ref,
    sh_ref, ng_ref,
    xv, gv, wv, cv, rs, rsr, xr, acc, ps, pr, lo, pgv, gp, rb,
    lsem, wsem,
    st_s, st_r, x_s, x_r, p_s, p_r, g_s, g_r, sh_s, sh_r,
    a_s, a_r, r_s, r_r, c_s, c_r,
):
    p = lax.axis_index("pipe")
    d = lax.axis_index("dp")
    t = lax.axis_index("tensor")
    T, D = x_ref.shape[1], x_ref.shape[2]
    K, C = w_ref.shape[1], w_ref.shape[2]
    KC, KQ, TB = K // NS, K // nt, T // NB

    def remote(src, dst, ss, rsem, **dev):
        return pltpu.make_async_remote_copy(
            src_ref=src, dst_ref=dst, send_sem=ss, recv_sem=rsem,
            device_id=dev, device_id_type=MESH,
        )

    nxt, prv = lax.rem(p + 1, np_), lax.rem(p + np_ - 1, np_)
    barrier = pltpu.get_barrier_semaphore()
    for o in range(1, nd):
        pl.semaphore_signal(barrier, inc=1, device_id={"dp": lax.rem(d + o, nd)}, device_id_type=MESH)
    for o in range(1, nt):
        pl.semaphore_signal(barrier, inc=1, device_id={"tensor": lax.rem(t + o, nt)}, device_id_type=MESH)
    pl.semaphore_signal(barrier, inc=1, device_id={"pipe": nxt}, device_id_type=MESH)
    pl.semaphore_signal(barrier, inc=1, device_id={"pipe": prv}, device_id_type=MESH)

    cx = pltpu.make_async_copy(x_ref.at[0], xv, lsem.at[0])
    cg = pltpu.make_async_copy(g_ref, gv, lsem.at[1])
    cc = pltpu.make_async_copy(c_ref.at[0], cv, lsem.at[2])
    cx.start()
    cg.start()
    cws = [
        pltpu.make_async_copy(w_ref.at[0, pl.ds(k * KC, KC)], wv.at[pl.ds(k * KC, KC)], wsem.at[k])
        for k in range(NS)
    ]
    for cw in cws:
        cw.start()
    cc.start()

    def peer(o):
        return lax.rem(d + o, nd)

    xcp = [[[
        remote(
            xv.at[pl.ds(b * TB, TB), pl.ds(pl.multiple_of(peer(o) * K + k * KC, 128), KC)],
            xr.at[o - 1, pl.ds(b * TB, TB), pl.ds(k * KC, KC)],
            x_s.at[b, o - 1, k], x_r.at[b, o - 1, k], dp=peer(o),
        ) for o in range(1, nd)] for k in range(NS)] for b in range(NB)]
    stcp = [
        remote(rs, rsr.at[o - 1], st_s.at[o - 1], st_r.at[o - 1], dp=peer(o)) for o in range(1, nd)
    ]
    pcp = [[
        remote(
            ps.at[b, nd - o - 1], pr.at[b, o - 1], p_s.at[b, o - 1], p_r.at[b, o - 1], dp=peer(o)
        ) for o in range(1, nd)] for b in range(NB)]
    gcp = [[
        remote(
            pgv.at[b, 0], pgv.at[b, o], g_s.at[b, o - 1], g_r.at[b, o - 1], dp=peer(o)
        ) for o in range(1, nd)] for b in range(NB)]
    shcp = [
        remote(lo.at[b], sh_ref.at[0, pl.ds(b * TB, TB)], sh_s.at[b], sh_r.at[b], pipe=nxt)
        for b in range(NB)
    ]

    def start_x(b, ks):
        for k in ks:
            for cp in xcp[b][k]:
                cp.start()

    cx.wait()
    ss = jnp.zeros((T, 1), F32)
    SC = D // 8
    for k in range(8):
        xf = xv[:, k * SC:(k + 1) * SC].astype(F32)
        ss = ss + jnp.sum(xf * xf, axis=-1, keepdims=True)
    scale = lax.rsqrt(ss * (1.0 / D) + 1e-05)
    rs[...] = jnp.broadcast_to(scale, rs.shape)

    pl.semaphore_wait(barrier, (nd - 1) + (nt - 1) + 2)

    start_x(0, range(NS))
    for cp in stcp:
        cp.start()
    start_x(1, range(2))

    cg.wait()

    def gain(k):
        return gv[:, pl.ds(pl.multiple_of(d * K + k * KC, 128), KC)]

    for k in range(NS):
        xf = xv[:, pl.ds(pl.multiple_of(d * K + k * KC, 128), KC)].astype(F32)
        nb = (xf * rs[:, 0:1] * gain(k)).astype(BF16)
        cws[k].wait()
        part = jnp.dot(nb, wv[k * KC:(k + 1) * KC, :], preferred_element_type=F32)
        if k == 0:
            acc[0] = part
        else:
            acc[0] += part
    for cp in stcp:
        cp.wait_recv()
    cc.wait()

    def project_peers(b):
        rows = slice(b * TB, (b + 1) * TB)
        for k in range(NS):
            for o in range(1, nd):
                xcp[b][k][o - 1].wait_recv()
                xf = xr[o - 1, rows, k * KC:(k + 1) * KC].astype(F32)
                nb = (xf * rsr[o - 1, rows, 0:1] * gain(k)).astype(BF16)
                part = jnp.dot(nb, wv[k * KC:(k + 1) * KC, :], preferred_element_type=F32)
                if k == 0:
                    acc[o, rows] = part
                elif k < NS - 1:
                    acc[o, rows] += part
                else:
                    ps[b, o - 1] = (acc[o, rows] + part).astype(BF16)
                    pcp[b][nd - o - 1].start()

    k0 = 0.7978845608028654
    k1 = 0.044715
    CB = 256

    def activate(b):
        rows = slice(b * TB, (b + 1) * TB)
        for cp in pcp[b]:
            cp.wait_recv()
        for i in range(C // CB):
            cols = slice(i * CB, (i + 1) * CB)
            pre = acc[0, rows, cols].astype(BF16).astype(F32)
            for o in range(1, nd):
                pre = pre + pr[b, o - 1, :, cols].astype(F32)
            sq = pre * pre
            th = jnp.tanh(k0 * (pre + k1 * (sq * pre)))
            cdf = 0.5 * (1.0 + th)
            slope = cdf + 0.5 * pre * ((1.0 - th * th) * (k0 * (1.0 + 3.0 * k1 * sq)))
            pgv[b, 0, :, cols] = (cv[rows, cols].astype(F32) * slope).astype(BF16)
            res = xv[rows, pl.ds(pl.multiple_of(t * C + i * CB, 128), CB)].astype(F32)
            lo[b, :, cols] = (res + pre * cdf).astype(BF16)
        for cp in gcp[b]:
            cp.start()
        shcp[b].start()

    low = t < 2
    inner = jnp.where(low, 1, 2)
    outer = jnp.where(low, 0, 3)
    is_outer = t == outer
    is_inner = t == inner
    partner = inner + outer - t
    dests = [3 - outer, 3 - inner, partner, t]
    acp, rcp, ccp = [], [], []
    for s in range(NB):
        acp.append(remote(gp.at[s, 2], rb.at[s, 0], a_s.at[s], a_r.at[s], tensor=partner))
        rcp.append([remote(gp.at[s, j], rb.at[s, 2 + j], r_s.at[s, j], r_r.at[s, j], tensor=partner) for j in range(2)])
        ccp.append([remote(gp.at[s, j], rb.at[s, 1], c_s.at[s, j], c_r.at[s], tensor=dests[j]) for j in range(2)])

    def input_grad(b):
        for cp in gcp[b]:
            cp.wait_recv()
        for j in range(4):
            pg = pgv[b].reshape(nd * TB, C)
            wb = wv[pl.ds(pl.multiple_of(dests[j] * KQ, KQ), KQ), :]
            part = lax.dot_general(pg, wb, (((1,), (1,)), ((), ())), preferred_element_type=F32)
            gp[b, j] = part.astype(BF16)
            if j < 2:
                @pl.when(is_outer)
                def _():
                    rcp[b][j].start()
            elif j == 2:
                acp[b].start()

    def relay(b, j):
        @pl.when(is_inner)
        def _():
            rcp[b][j].wait_recv()
            gp[b, j] = (gp[b, j].astype(F32) + rb[b, 2 + j].astype(F32)).astype(BF16)
            ccp[b][j].start()

    def finish(b):
        acp[b].wait_recv()
        ccp[b][0].wait_recv()
        for o in range(nd):
            r = slice(o * TB, (o + 1) * TB)
            row = pl.multiple_of(lax.rem(d - o + nd, nd) * T + b * TB, TB)
            ng_ref[0, pl.ds(row, TB), :] = (
                gp[b, 3, r].astype(F32) + rb[b, 0, r].astype(F32) + rb[b, 1, r].astype(F32)
            ).astype(BF16)

    project_peers(0)
    start_x(1, range(2, NS))
    activate(0)
    project_peers(1)
    input_grad(0)
    activate(1)
    relay(0, 0)
    input_grad(1)
    relay(0, 1)
    relay(1, 0)
    relay(1, 1)
    finish(0)
    finish(1)

    for b in range(NB):
        for k in range(NS):
            for cp in xcp[b][k]:
                cp.wait_send()
        for cp in pcp[b] + gcp[b]:
            cp.wait_send()
        acp[b].wait_send()
        shcp[b].wait()
    for cp in stcp:
        cp.wait_send()

    @pl.when(is_outer)
    def _():
        for s in range(NB):
            for j in range(2):
                rcp[s][j].wait_send()

    @pl.when(is_inner)
    def _():
        for s in range(NB):
            for j in range(2):
                ccp[s][j].wait_send()


def place(a_ref, b_ref, oa_ref, ob_ref):
    oa_ref[...] = a_ref[...]
    ob_ref[...] = b_ref[...]


def per_device(np_, nd, nt, x, g, w, c):
    T, D = x.shape[1:]
    K, C = w.shape[1:]
    KQ, TB = K // nt, T // NB
    o = nd - 1
    dma = pltpu.SemaphoreType.DMA
    scratch = [
        pltpu.VMEM((T, D), BF16),
        pltpu.VMEM((1, D), F32),
        pltpu.VMEM((K, C), BF16),
        pltpu.VMEM((T, C), BF16),
        pltpu.VMEM((T, 128), F32),
        pltpu.VMEM((o, T, 128), F32),
        pltpu.VMEM((o, T, K), BF16),
        pltpu.VMEM((nd, T, C), F32),
        pltpu.VMEM((NB, o, TB, C), BF16),
        pltpu.VMEM((NB, o, TB, C), BF16),
        pltpu.VMEM((NB, TB, C), BF16),
        pltpu.VMEM((NB, nd, TB, C), BF16),
        pltpu.VMEM((NB, 4, nd * TB, KQ), BF16),
        pltpu.VMEM((NB, 4, nd * TB, KQ), BF16),
        dma((3,)), dma((NS,)),
        dma((o,)), dma((o,)), dma((NB, o, NS)), dma((NB, o, NS)), dma((NB, o)), dma((NB, o)),
        dma((NB, o)), dma((NB, o)), dma((NB,)), dma((NB,)),
        dma((NB,)), dma((NB,)), dma((NB, 2)), dma((NB, 2)), dma((NB, 2)), dma((NB,)),
    ]
    vmem = pl.BlockSpec(memory_space=pltpu.VMEM)
    hbm = pl.BlockSpec(memory_space=pl.ANY)
    shifted, grad = pl.pallas_call(
        functools.partial(kernel, np_, nd, nt),
        out_shape=(
            jax.ShapeDtypeStruct((1, T, C), BF16),
            jax.ShapeDtypeStruct((1, T * nd, KQ), BF16),
        ),
        in_specs=[hbm] * 4,
        out_specs=(hbm, pl.BlockSpec(memory_space=pltpu.VMEM)),
        scratch_shapes=scratch,
        compiler_params=pltpu.CompilerParams(
            collective_id=0, has_side_effects=True, vmem_limit_bytes=58 * 2**20
        ),
        cost_estimate=pl.CostEstimate(
            flops=4 * T * nd * K * C, bytes_accessed=2 * K * C + 4 * T * D, transcendentals=T * C
        ),
    )(x, g, w, c)
    return pl.pallas_call(
        place,
        out_shape=(
            jax.ShapeDtypeStruct(shifted.shape, BF16),
            jax.ShapeDtypeStruct(grad.shape, BF16),
        ),
        in_specs=[vmem] * 2,
        out_specs=(vmem, vmem),
    )(shifted, grad)


def solution(mesh):
    in_specs = (
        P("pipe", "dp", None),
        P("pipe", None),
        P("pipe", "dp", "tensor"),
        P("pipe", "dp", "tensor"),
    )
    out_specs = (P("pipe", "dp", "tensor"), P("pipe", None, ("dp", "tensor")))
    body = functools.partial(per_device, mesh.shape["pipe"], mesh.shape["dp"], mesh.shape["tensor"])
    return jax.shard_map(body, mesh=mesh, in_specs=in_specs, out_specs=out_specs, check_vma=False)
```
